128 devices in a mesh: seq: 8 (over z, core), tp: 16 (over x, y).
Axes of the slice: x: 4, y: 4, z: 4, core: 2. Of those that a mesh axis runs over, the one named last changes fastest.
Arguments:
- temporal: bfloat16 [12288, 4096], P('seq', 'tp'), may hold values from -6 to 6
- w_in: bfloat16 [4096, 1024], P('tp'), may hold values from -0.09375 to 0.09375
- audio_mask: int32 [12288], P('seq'), may hold values from 0 to 1, as said below
- counts: int32 [128], replicated, may hold values from 8 to 88, as said below
- codes: int32 [12288, 8], P(('seq', 'tp')), may hold values from 0 to 2047
- cotangent: bfloat16 [12288, 8, 1024], P(('seq', 'tp')), may hold values from -1.5 to 1.5
- norm_gain: float32 [1024], replicated, may hold values from 0.5 to 1.5
- w_qkv: bfloat16 [1024, 3072], replicated, may hold values from -8 to 8
- w_out: bfloat16 [1024, 1024], replicated, may hold values from -0.1875 to 0.1875
- adapter_a: bfloat16 [8, 2048, 128], replicated, may hold values from -6 to 6
- adapter_b: bfloat16 [8, 128, 1024], replicated, may hold values from -0.5 to 0.5
Outputs:
- grad_temporal: bfloat16 [12288, 4096], P('seq', 'tp')
- grad_w_in: float32 [4096, 1024], P('tp', 'seq')
- grad_norm_gain: float32 [1024], P(('seq', 'tp'))
- grad_w_qkv: float32 [1024, 3072], P(('seq', 'tp'))
- grad_w_out: float32 [1024, 1024], P(('seq', 'tp'))
- grad_adapter_a: float32 [8, 2048, 128], P(None, ('seq', 'tp'))
- grad_adapter_b: float32 [8, 128, 1024], P(None, ('seq', 'tp'))
The draws below stay inside these ranges and needn't reach their ends.
Inputs may be any that keep to these rules, and one draw needn't show every extreme that they name: In every block of 96 frames the ones of audio_mask number counts of that block. counts[b] is the number of audio frames among frames b * 96 to (b + 1) * 96 - 1; for s < 8 and t < 8 the blocks s * 16 + t and s * 16 + t + 8 hold 96 audio frames together; some block holds exactly 88.
All inputs are finite; a program needn't handle non-finite values.
Results may differ from the reference program's by a relative error of at most 0.012.
The reference program's roundings to bfloat16 on the way count: a program that leaves them out, or rounds other values in their place, can miss the bound.
Values may be sent and summed in bfloat16 or wider, within the bound.
No kernel may reach another device: no remote copies, remote signals or barrier semaphores. Data moves between devices by JAX's collectives and lax.ppermute only.
A program may use at most 128 MiB of HBM per device.

```python
import math
import jax
import jax.numpy as jnp
from jax import lax

D = 1024
TEMP_D = 4096
CODEBOOKS = 8
VOCAB = 2048
RANK = 128
HEADS = 16
HEAD_DIM = 64
BLOCK = 96
AUDIO = 48
PEAK = 88
FRAMES = 12288
N_SEQ = 8
N_TP = 16


def block_counts(key):
    halfway = N_TP // 2
    pairs = N_SEQ * halfway
    heavy = jax.random.randint(jax.random.fold_in(key, 1), (pairs,), AUDIO, PEAK + 1)
    fullest = jax.random.randint(jax.random.fold_in(key, 2), (), 0, pairs)
    heavy = jnp.where(jnp.arange(pairs) == fullest, PEAK, heavy)
    flipped = jax.random.randint(jax.random.fold_in(key, 3), (pairs,), 0, 2) == 1
    light = 2 * AUDIO - heavy
    first = jnp.where(flipped, heavy, light).reshape(N_SEQ, halfway)
    second = jnp.where(flipped, light, heavy).reshape(N_SEQ, halfway)
    return jnp.concatenate([first, second], axis=1).reshape(N_SEQ * N_TP).astype(jnp.int32)


def block_order(single):
    return jax.random.permutation(single, BLOCK)


def draw_counts(key, part):
    return block_counts(key)


def draw_audio_mask(key, part):
    amounts = block_counts(key)
    key = jax.random.fold_in(key, 7)
    blocks = N_SEQ * N_TP
    orders = jax.vmap(block_order)(jax.random.split(key, blocks))
    return (orders < amounts[:, None]).astype(jnp.int32).reshape(blocks * BLOCK)


def draw_w_qkv(key, part):
    key = jax.random.fold_in(key, 21)
    base = jax.random.normal(key, (D, 3 * D), jnp.float32) * D ** (-0.5)
    return base.astype(jnp.bfloat16)


def plant(entries, rng, low, high):
    longest = entries.shape.index(max(entries.shape))
    spots = []
    for shift in (0, 1):
        where = [jax.random.randint(jax.random.fold_in(rng, axis), (), 0, length) for axis, length in enumerate(entries.shape)]
        where[longest] = (where[longest] + shift) % entries.shape[longest]
        spots.append(tuple(where))
    return entries.at[spots[0]].set(low).at[spots[1]].set(high)


def shard_levels(key, shape, shards, smallest, top_value):
    factor_of, own = 1.0, jax.random.fold_in(key, 6)
    for dim, shards_of in shards:
        heights = jnp.exp(jax.random.uniform(jax.random.fold_in(own, dim), (shards_of,), jnp.float32, smallest / len(shards), top_value / len(shards)))
        factor_of = factor_of * jnp.repeat(heights, shape[dim] // shards_of).reshape([-1 if axis == dim else 1 for axis in range(len(shape))])
    return factor_of


def bell_draw(own_key, shape, deviation, bound, pieces=(), kind=jnp.bfloat16):
    factor_of = shard_levels(own_key, shape, pieces, -0.22, 0.18) if pieces else 1.0
    values = jax.random.normal(own_key, shape, jnp.float32) * deviation * factor_of
    return jnp.minimum(jnp.maximum(values, -bound), bound).astype(kind)


def setup_inputs(seed: int = 0) -> dict:
    seeds = jax.random.split(jax.random.key(seed), 12)
    temporal = bell_draw(seeds[0], (FRAMES, TEMP_D), 1.0, 6.0, ((0, 8), (1, 16)))
    w_in = bell_draw(seeds[1], (TEMP_D, D), TEMP_D ** -0.5, 0.09375, ((0, 16),))
    audio_mask = draw_audio_mask(jax.random.fold_in(seeds[11], 71), 0)
    counts = draw_counts(jax.random.fold_in(seeds[11], 71), 0)
    codes = plant(jax.random.randint(seeds[4], (FRAMES, CODEBOOKS), 0, VOCAB), jax.random.fold_in(seeds[4], 1), 0, VOCAB - 1).astype(jnp.int32)
    cotangent = bell_draw(seeds[5], (FRAMES, CODEBOOKS, D), 0.25, 1.5, ((0, 128),))
    norm_gain = jnp.clip(1.0 + 0.1 * jax.random.normal(seeds[6], (D,), jnp.float32), 0.5, 1.5)
    w_qkv = draw_w_qkv(jax.random.fold_in(seeds[11], 71), 0)
    w_out = bell_draw(seeds[8], (D, D), D ** -0.5, 0.1875)
    adapter_a = bell_draw(seeds[9], (CODEBOOKS, VOCAB, RANK), 1.0, 6.0)
    adapter_b = bell_draw(seeds[10], (CODEBOOKS, RANK, D), RANK ** -0.5, 0.5)
    return {"temporal": temporal, "w_in": w_in, "audio_mask": audio_mask, "counts": counts, "codes": codes, "cotangent": cotangent, "norm_gain": norm_gain, "w_qkv": w_qkv, "w_out": w_out, "adapter_a": adapter_a, "adapter_b": adapter_b}


def rounded(value):
    return lax.optimization_barrier(value.astype(jnp.bfloat16))

def attention_backward(proj, low, upstream, weight, norm_gain, w_qkv, w_out, adapter_b):
    number = proj.shape[0]
    embedded = jnp.einsum('rkc,kcd->rkd', low.astype(jnp.float32), adapter_b.astype(jnp.float32))
    stream = proj.astype(jnp.float32)[:, None, :] + embedded
    inv_rms = lax.rsqrt(lax.optimization_barrier(jnp.mean(stream * stream, axis=-1, keepdims=True)) + 1e-05)
    normed = rounded(stream * inv_rms * norm_gain)
    flat = normed.reshape(number * CODEBOOKS, D)
    packed = rounded(jnp.dot(flat, w_qkv, preferred_element_type=jnp.float32))
    packed = packed.reshape(number, CODEBOOKS, 3, HEADS, HEAD_DIM).astype(jnp.float32)
    query = packed[:, :, 0]
    keys = packed[:, :, 1]
    values = packed[:, :, 2]
    scale = 1.0 / math.sqrt(HEAD_DIM)
    scores = jnp.einsum('rqhe,rkhe->rhqk', query, keys) * scale
    causal = jnp.arange(CODEBOOKS)[:, None] >= jnp.arange(CODEBOOKS)[None, :]
    scores = jnp.where(causal, scores, -1e+30)
    probs = jax.nn.softmax(scores, axis=-1)
    probs_low = rounded(probs).astype(jnp.float32)
    mixed = rounded(jnp.einsum('rhqk,rkhe->rqhe', probs_low, values)).reshape(number * CODEBOOKS, D)
    grad_out = upstream.astype(jnp.float32) * weight[:, None, None]
    grad_low = rounded(grad_out).reshape(number * CODEBOOKS, D)
    grad_wout = jnp.dot(mixed.T, grad_low, preferred_element_type=jnp.float32)
    grad_mixed = rounded(jnp.dot(grad_low, w_out.T, preferred_element_type=jnp.float32))
    grad_mixed = grad_mixed.reshape(number, CODEBOOKS, HEADS, HEAD_DIM).astype(jnp.float32)
    grad_probs = jnp.einsum('rqhe,rkhe->rhqk', grad_mixed, values)
    grad_values = rounded(jnp.einsum('rhqk,rqhe->rkhe', probs_low, grad_mixed))
    inner = lax.optimization_barrier(jnp.sum(probs * grad_probs, axis=-1, keepdims=True))
    grad_scores = rounded(probs * (grad_probs - inner) * scale).astype(jnp.float32)
    grad_query = rounded(jnp.einsum('rhqk,rkhe->rqhe', grad_scores, keys))
    grad_keys = rounded(jnp.einsum('rhqk,rqhe->rkhe', grad_scores, query))
    grad_packed = jnp.stack([grad_query, grad_keys, grad_values], axis=2).reshape(number * CODEBOOKS, 3 * D)
    grad_wqkv = jnp.dot(flat.T, grad_packed, preferred_element_type=jnp.float32)
    grad_normed = jnp.dot(grad_packed, w_qkv.T, preferred_element_type=jnp.float32).reshape(number, CODEBOOKS, D)
    grad_gain = lax.optimization_barrier(jnp.sum(grad_normed * stream * inv_rms, axis=(0, 1)))
    scaled = grad_normed * norm_gain
    grad_stream = grad_out + inv_rms * (scaled - stream * inv_rms * inv_rms * lax.optimization_barrier(jnp.mean(scaled * stream, axis=-1, keepdims=True)))
    return (grad_stream, (grad_gain, grad_wqkv, grad_wout))

def reference(temporal, w_in, audio_mask, counts, codes, cotangent, norm_gain, w_qkv, w_out, adapter_a, adapter_b):
    total = AUDIO * N_SEQ * N_TP
    chosen = jnp.nonzero(audio_mask, size=total)[0].astype(jnp.int32)
    proj_all = rounded(jnp.dot(temporal, w_in, preferred_element_type=jnp.float32))
    book = jnp.arange(CODEBOOKS, dtype=jnp.int32)[None, :]

    def step(carry, frames):
        proj = proj_all[frames]
        tokens = codes[frames]
        low = adapter_a[book, tokens]
        weight = AUDIO / counts[frames // BLOCK].astype(jnp.float32)
        grad_stream, grads = attention_backward(proj, low, cotangent[frames], weight, norm_gain, w_qkv, w_out, adapter_b)
        grad_proj = lax.optimization_barrier(jnp.sum(grad_stream, axis=1)).astype(jnp.bfloat16)
        stream_low = rounded(grad_stream).astype(jnp.float32)
        grad_b = jnp.einsum('rkc,rkd->kcd', low.astype(jnp.float32), stream_low)
        grad_lowrank = rounded(jnp.einsum('rkd,kcd->rkc', stream_low, adapter_b.astype(jnp.float32)))
        grad_a = carry[3].at[book, tokens].add(grad_lowrank.astype(jnp.float32))
        updated = (carry[0] + grads[0], carry[1] + grads[1], carry[2] + grads[2], grad_a, carry[4] + grad_b)
        return (updated, grad_proj)
    start = (jnp.zeros((D,), jnp.float32), jnp.zeros((D, 3 * D), jnp.float32), jnp.zeros((D, D), jnp.float32), jnp.zeros((CODEBOOKS, VOCAB, RANK), jnp.float32), jnp.zeros((CODEBOOKS, RANK, D), jnp.float32))
    sums, grad_proj = lax.scan(step, start, chosen.reshape(N_SEQ, total // N_SEQ))
    full = jnp.zeros((FRAMES, D), jnp.bfloat16).at[chosen].set(grad_proj.reshape(total, D))
    grad_temporal = jnp.dot(full, w_in.T, preferred_element_type=jnp.float32).astype(jnp.bfloat16)
    grad_win = jnp.dot(temporal.T, full, preferred_element_type=jnp.float32)
    return (grad_temporal, grad_win, sums[0], sums[1], sums[2], sums[3], sums[4])
```

```python
import math

import jax
import jax.numpy as jnp
from jax import lax
from jax.experimental import pallas as pl
from jax.experimental.pallas import tpu as pltpu
from jax.sharding import Mesh, PartitionSpec as P

HEADS = 16
AUDIO = 48
EXTRA = 40
BLOCK = 96
BOOKS = 8
RANK = 128
GROUP = 16
GROUPS = AUDIO // GROUP
ROWS = AUDIO * BOOKS
SPAN = GROUP * BOOKS
TPS = 16
WIDTH = 1024
VOCAB = 2048
LEFT = 3 * WIDTH
GAIN = 128
RIGHT = 5 * WIDTH + GAIN - LEFT
TABLE = VOCAB
F32 = jnp.float32
BF16 = jnp.bfloat16
I32 = jnp.int32
NT = (((1,), (1,)), ((), ()))
TN = (((0,), (0,)), ((), ()))
MIB = 1024 * 1024


def dot(a, b, dims=None):
    if dims is None:
        return jnp.dot(a, b, preferred_element_type=F32)
    return lax.dot_general(a, b, dims, preferred_element_type=F32)


def iota(shape, dim):
    return lax.broadcasted_iota(I32, shape, dim)


def ones_where(cond):
    return jnp.where(cond, 1.0, 0.0).astype(BF16)


def shaped(*shape, dtype=BF16):
    return jax.ShapeDtypeStruct(shape, dtype)


def call(kernel, name, out, args, scalars=0, scratch=(), limit=12):
    vmem = pl.BlockSpec(memory_space=pltpu.VMEM)
    smem = pl.BlockSpec(memory_space=pltpu.SMEM)
    return pl.pallas_call(
        kernel,
        out_shape=out,
        in_specs=[smem] * scalars + [vmem] * (len(args) - scalars),
        out_specs=jax.tree.map(lambda _: vmem, out),
        scratch_shapes=list(scratch),
        compiler_params=pltpu.CompilerParams(vmem_limit_bytes=limit * MIB),
        cost_estimate=pl.CostEstimate(flops=0, bytes_accessed=0, transcendentals=0),
        name=name,
    )(*args)


def ranks(mask_ref):
    mask = mask_ref[...].astype(F32)
    before = ones_where(iota((BLOCK, BLOCK), 0) < iota((BLOCK, BLOCK), 1))
    rank = dot(mask.astype(BF16), before)
    return mask > 0, rank, jnp.sum(mask, axis=1, keepdims=True)


def own_row(a, column):
    a = jnp.broadcast_to(a, (TPS, a.shape[1]))
    return jnp.sum(jnp.where(iota(a.shape, 0) == column, a, 0.0), axis=0, keepdims=True)


def each_book(row):
    spread = ones_where(iota((BLOCK, BLOCK * BOOKS), 1) // BOOKS == iota((BLOCK, BLOCK * BOOKS), 0))
    wide = dot(jnp.broadcast_to(row, (8, BLOCK)).astype(BF16), spread)
    return wide[:1].astype(I32)


def select_codes(chosen, codes):
    high = dot(chosen, (codes >> 6).astype(F32).astype(BF16))
    low = dot(chosen, (codes & 63).astype(F32).astype(BF16))
    return high.astype(I32) * 64 + low.astype(I32)


def project_kernel(
    place, mask, temporal, w_in, codes, o0, o1, o2, o3, chosen, keeps_o, goes_o, code_o, rows
):
    audio, rank, count = ranks(mask)
    leaves = own_row(jnp.where(audio & (rank >= AUDIO), rank - AUDIO, -1.0), place[4])
    code_o[...] = select_codes(ones_where(leaves.astype(I32) == iota((EXTRA, BLOCK), 0)), codes[...])
    keeps = jnp.where(audio & (rank < AUDIO), rank, -1.0).astype(I32)
    goes = jnp.where(audio & (rank >= AUDIO), rank + AUDIO - count, -1.0).astype(I32)
    keeps_o[...] = keeps
    goes_o[...] = goes
    slots = iota((AUDIO, BLOCK), 0)
    for b in range(TPS):
        o = b ^ 8
        mine = dot(ones_where(keeps[b : b + 1] == slots), temporal[b * BLOCK : (b + 1) * BLOCK, :])
        theirs = dot(ones_where(goes[o : o + 1] == slots), temporal[o * BLOCK : (o + 1) * BLOCK, :])
        chosen[b * AUDIO : (b + 1) * AUDIO, :] = (mine + theirs).astype(BF16)
    for d, out in enumerate((o0, o1, o2, o3)):
        for x in range(4):
            source = pl.ds(pl.multiple_of((x * 4 + (place[3] ^ d)) * AUDIO, AUDIO), AUDIO)
            rows[x * AUDIO : (x + 1) * AUDIO, :] = chosen[source, :]
        out[...] = dot(rows[...], w_in[...]).astype(out.dtype)


def project_meet_kernel(place, p0, p1, p2, p3, o0, o1, o2, o3, total):
    total[...] = p0[...] + p1[...].astype(F32) + p2[...].astype(F32) + p3[...].astype(F32)
    for d, out in enumerate((o0, o1, o2, o3)):
        rows = pl.ds(pl.multiple_of((place[2] ^ d) * AUDIO, AUDIO), AUDIO)
        out[...] = total[rows, :].astype(out.dtype)


def leave_kernel(place, mask, cot, cot_o):
    audio, rank, _ = ranks(mask)
    row = own_row(jnp.where(audio & (rank >= AUDIO), rank - AUDIO, -1.0), place[4])
    wide = each_book(row)
    key = jnp.where(wide >= 0, wide * BOOKS + iota(wide.shape, 1) % BOOKS, -1)
    spread = ones_where(key == iota((EXTRA * BOOKS, BLOCK * BOOKS), 0))
    for i in range(2):
        cols = slice(i * 512, (i + 1) * 512)
        cot_o[:, cols] = dot(spread, cot[:, cols]).astype(BF16)


def embed_kernel(place, mask, codes, codes_come, table, adapter_b, tokens_o, low_o, embedded_o):
    audio, rank, count = ranks(mask)
    row = own_row(jnp.where(audio & (rank < AUDIO), rank, -1.0), place[4]).astype(I32)
    have = own_row(count, place[4]).astype(I32)
    comes = jnp.broadcast_to(have, (1, EXTRA)) + iota((1, EXTRA), 1)
    tokens = select_codes(ones_where(row == iota((AUDIO, BLOCK), 0)), codes[...])
    tokens = tokens + select_codes(ones_where(comes == iota((AUDIO, EXTRA), 0)), codes_come[...])
    tokens_o[...] = tokens
    vocab = iota((AUDIO, VOCAB), 1)
    for k in range(BOOKS):
        rows = slice(k * AUDIO, (k + 1) * AUDIO)
        low = dot(ones_where(tokens[:, k : k + 1] == vocab), table[k]).astype(BF16)
        low_o[rows, :] = low
        embedded_o[rows, :] = dot(low, adapter_b[k])


def upstream_kernel(place, mask, cot, cot_come, w_out, cot_o, weights_o, grad_low_o, grad_mixed_o):
    audio, rank, count = ranks(mask)
    row = own_row(jnp.where(audio & (rank < AUDIO), rank, -1.0), place[4])
    have = own_row(count, place[4])
    slot = iota((ROWS, 128), 0)
    slot = (slot // SPAN) * GROUP + slot % GROUP
    weights = jnp.where(slot < have.astype(I32), AUDIO / have, AUDIO / (BLOCK - have))
    weights_o[...] = weights

    def target(at, book):
        return jnp.where((at >= 0) & (at < AUDIO), (at // GROUP) * SPAN + book * GROUP + at % GROUP, -1)

    wide = each_book(row)
    stays = ones_where(target(wide, iota(wide.shape, 1) % BOOKS) == iota((ROWS, BLOCK * BOOKS), 0))
    index = iota((1, EXTRA * BOOKS), 1)
    come = jnp.broadcast_to(have.astype(I32), index.shape) + index // BOOKS
    comes = ones_where(target(come, index % BOOKS) == iota((ROWS, EXTRA * BOOKS), 0))
    for i in range(2):
        cols = slice(i * 512, (i + 1) * 512)
        here = dot(stays, cot[:, cols]) + dot(comes, cot_come[:, cols])
        cot_o[:, cols] = here.astype(BF16)
        grad_low_o[:, cols] = (here * weights[:, :1]).astype(BF16)
    for i in range(4):
        cols = slice(i * 256, (i + 1) * 256)
        grad_mixed_o[:, cols] = dot(grad_low_o[...], w_out[cols, :], NT).astype(BF16)


def split(a):
    first = iota((SPAN, 128), 1) < 64
    zero = jnp.zeros_like(a)
    return jnp.concatenate([jnp.where(first, a, zero), jnp.where(first, zero, a)], axis=0)


def pick(a):
    return jnp.where(iota((SPAN, 128), 1) < 64, a[:SPAN], a[SPAN:])


def pair_columns(part, p):
    return pl.ds(pl.multiple_of(part * WIDTH + p * 128, 128), 128)


def pair_probs(p, g):
    return pl.ds(pl.multiple_of((p * GROUPS + g) * SPAN, SPAN), SPAN)


SCALE = 1.0 / math.sqrt(64)


def forward_kernel(
    p0, p1, p2, p3, embedded, gain, w_qkv, normed_o, mixed_o, packed_o, stream_o, inv_o, probs_o
):
    for g in range(GROUPS):
        frames = pl.ds(g * GROUP, GROUP)
        proj = p0[frames, :] + p1[frames, :].astype(F32) + p2[frames, :].astype(F32) + p3[frames, :].astype(F32)
        proj = proj.astype(BF16).astype(F32)
        for k in range(BOOKS):
            rows = pl.ds(g * SPAN + k * GROUP, GROUP)
            x = proj + embedded[pl.ds(k * AUDIO + g * GROUP, GROUP), :]
            stream_o[rows, :] = x
            a = lax.rsqrt(jnp.mean(x * x, axis=-1, keepdims=True) + 1e-05)
            inv_o[rows, :] = jnp.broadcast_to(a, (GROUP, 128))
            normed_o[rows, :] = (x * a * gain[...]).astype(BF16)

    tile = 512

    @pl.loop(0, 3 * WIDTH // tile)
    def _(i):
        cols = pl.ds(pl.multiple_of(i * tile, tile), tile)
        packed_o[:, cols] = dot(normed_o[...], w_qkv[:, cols]).astype(BF16)

    key_row = iota((SPAN, 2 * SPAN), 0)
    query_row = iota((SPAN, 2 * SPAN), 1) % SPAN
    allowed = (key_row % GROUP == query_row % GROUP) & (key_row // GROUP <= query_row // GROUP)

    @pl.loop(0, HEADS // 8)
    def _(half):
        for p, g in ((half * 4 + i, g) for i in range(4) for g in range(GROUPS)):
            rows = pl.ds(g * SPAN, SPAN)
            query = split(packed_o[rows, pair_columns(0, p)])
            keys = packed_o[rows, pair_columns(1, p)]
            values = packed_o[rows, pair_columns(2, p)]
            scores = jnp.where(allowed, dot(keys, query, NT) * SCALE, -1e30)
            top = jnp.max(scores, axis=0, keepdims=True)
            e = jnp.exp(scores - top)
            probs = e * (1.0 / jnp.sum(e, axis=0, keepdims=True))
            probs_o[pair_probs(p, g), :] = probs
            mixed = pick(dot(probs.astype(BF16), values, TN))
            mixed_o[rows, pair_columns(0, p)] = mixed.astype(BF16)


def backward_kernel(packed, probs_in, grad_mixed, packed_grad_o):
    @pl.loop(0, HEADS // 8)
    def _(half):
        for p, g in ((half * 4 + i, g) for i in range(4) for g in range(GROUPS)):
            rows = pl.ds(g * SPAN, SPAN)
            query = split(packed[rows, pair_columns(0, p)])
            keys = packed[rows, pair_columns(1, p)]
            values = packed[rows, pair_columns(2, p)]
            gm = split(grad_mixed[rows, pair_columns(0, p)])
            probs = probs_in[pair_probs(p, g), :]
            grad_probs = dot(values, gm, NT)
            packed_grad_o[rows, pair_columns(2, p)] = dot(probs.astype(BF16), gm).astype(BF16)
            inner = jnp.sum(probs * grad_probs, axis=0, keepdims=True)
            grad_scores = (probs * (grad_probs - inner) * SCALE).astype(BF16)
            grad_query = pick(dot(grad_scores, keys, TN))
            packed_grad_o[rows, pair_columns(0, p)] = grad_query.astype(BF16)
            packed_grad_o[rows, pair_columns(1, p)] = dot(grad_scores, query).astype(BF16)


def norm_kernel(
    packed_grad, w_qkv, stream, inv, cot, weights, gain, adapter_b,
    tokens, message_o, stream_low_o, gain_o, grad_normed,
):
    tile = 256

    @pl.loop(0, WIDTH // tile)
    def _(i):
        cols = pl.ds(pl.multiple_of(i * tile, tile), tile)
        grad_normed[:, cols] = dot(packed_grad[...], w_qkv[cols, :], NT)

    gain_sum = jnp.zeros((GROUP, WIDTH), F32)
    for g in range(GROUPS):
        total = jnp.zeros((GROUP, WIDTH), F32)
        for k in range(BOOKS):
            rows = pl.ds(g * SPAN + k * GROUP, GROUP)
            x = stream[rows, :]
            a = inv[rows, :][:, :1]
            gn = grad_normed[rows, :]
            gain_sum = gain_sum + gn * (x * a)
            scaled = gn * gain[...]
            mean = jnp.mean(scaled * x, axis=-1, keepdims=True)
            grad_out = cot[rows, :].astype(F32) * weights[rows, :][:, :1]
            gs = grad_out + a * (scaled - x * (a * a * mean))
            total = total + gs
            stream_low_o[pl.ds(k * AUDIO + g * GROUP, GROUP), :] = gs.astype(BF16)
        message_o[pl.ds(g * GROUP, GROUP), :WIDTH] = total.astype(BF16)
    gain_row = jnp.sum(gain_sum, axis=0, keepdims=True)
    for i in range(WIDTH // 128):
        piece = jnp.broadcast_to(gain_row[:, i * 128 : (i + 1) * 128], (128, 128))
        gain_o[i * 128 : (i + 1) * 128, :] = jnp.transpose(piece)
    for k in range(BOOKS):
        rows = pl.ds(k * AUDIO, AUDIO)
        lowrank = dot(stream_low_o[rows, :], adapter_b[k], NT).astype(BF16)
        message_o[AUDIO:, k * RANK : (k + 1) * RANK] = lowrank
    marks = jnp.zeros((AUDIO, RANK), F32)
    for k in range(BOOKS):
        token = jnp.broadcast_to(tokens[:, k : k + 1], (AUDIO, RANK))
        lane = iota((AUDIO, RANK), 1)
        marks = jnp.where(lane == k, (token >> 6).astype(F32), marks)
        marks = jnp.where(lane == BOOKS + k, (token & 63).astype(F32), marks)
    message_o[:AUDIO, WIDTH:] = marks.astype(BF16)
    message_o[AUDIO:, WIDTH:] = jnp.zeros((AUDIO, RANK), BF16)


def columns_of(a, core, order):
    return [jnp.transpose(a[:, pl.ds(pl.multiple_of((z * 2 + core) * 128, 128), 128)]) for z in order]


def give_kernel(place, normed, packed_grad, out, lhs):
    for i, block in enumerate(columns_of(normed, 1 - place[1], range(4))):
        lhs[i * 128 : (i + 1) * 128, :] = block
    tile = 512
    for i in range(LEFT // tile):
        cols = slice(i * tile, (i + 1) * tile)
        r = dot(lhs[...], packed_grad[:, cols]).astype(BF16)
        for z in range(4):
            out[z, :, cols] = r[z * 128 : (z + 1) * 128]


def backward_give_kernel(place, packed, probs_in, grad_mixed, normed, packed_grad_o, give_o, lhs):
    backward_kernel(packed, probs_in, grad_mixed, packed_grad_o)
    give_kernel(place, normed, packed_grad_o, give_o, lhs)


def norm_give_kernel(
    place, packed_grad, w_qkv, stream, inv, cot, weights, gain, adapter_b, tokens, mixed, grad_low, low,
    message_o, stream_low_o, gain_o, give_o, grad_normed, lhs,
):
    norm_kernel(
        packed_grad, w_qkv, stream, inv, cot, weights, gain, adapter_b, tokens,
        message_o, stream_low_o, gain_o, grad_normed,
    )
    give_late_kernel(place, mixed, grad_low, low, stream_low_o, gain_o, give_o, lhs)


def keep_left_kernel(place, normed, packed_grad, got, l0, l1, l2, l3, lhs):
    outs = (l0, l1, l2, l3)
    order = [place[0] ^ d for d in range(4)]
    for i, block in enumerate(columns_of(normed, place[1], order)):
        lhs[i * 128 : (i + 1) * 128, :] = block
    tile = 512
    for i in range(LEFT // tile):
        cols = slice(i * tile, (i + 1) * tile)
        r = dot(lhs[...], packed_grad[:, cols])
        for d in range(4):
            total = r[d * 128 : (d + 1) * 128] + got[order[d], :, cols].astype(F32)
            outs[d][:, cols] = total.astype(outs[d].dtype)


def rank_rows(low, rank, book):
    chosen = dot(ones_where(rank == iota((512, RANK), 1)), low[...], NT)
    return jnp.where(iota((512, ROWS), 1) // AUDIO == book, chosen, 0.0).astype(BF16)


def give_late_kernel(place, mixed, grad_low, low, stream_low, gain_col, out, lhs):
    other = 1 - place[1]
    for i, block in enumerate(columns_of(mixed, other, range(4))):
        lhs[i * 128 : (i + 1) * 128, :] = block
    row = iota((512, 1), 0)
    lhs2 = rank_rows(low, (row // 128) * 32 + other * 16 + (row % 128) // 8, row % 8)
    tile = 512
    for j, (left, right) in enumerate(((lhs[...], grad_low), (lhs2, stream_low))):
        for i in range(WIDTH // tile):
            r = dot(left, right[:, i * tile : (i + 1) * tile]).astype(BF16)
            at = j * WIDTH + i * tile
            for z in range(4):
                out[z, :, at : at + tile] = r[z * 128 : (z + 1) * 128]
    for z in range(4):
        rows = pl.ds(pl.multiple_of((z * 2 + other) * 128, 128), 128)
        out[z, :, 2 * WIDTH :] = gain_col[rows, :].astype(BF16)


def keep_right_kernel(place, mixed, grad_low, low, stream_low, gain_col, got, r0, r1, r2, r3, lhs, square):
    outs = (r0, r1, r2, r3)
    core = place[1]
    for z, block in enumerate(columns_of(mixed, core, range(4))):
        lhs[z * 128 : (z + 1) * 128, :] = block
    row = iota((512, 1), 0)
    lhs2 = rank_rows(low, (row // 128) * 32 + core * 16 + (row % 128) // 8, row % 8)

    def give(z, total, cols):
        square[...] = total
        for d, out in enumerate(outs):
            rows = pl.ds(pl.multiple_of((place[2] ^ d) * 32, 32), 32)
            out[z, :, cols] = square[rows, :].astype(out.dtype)

    tile = 512
    for j, (left, right) in enumerate(((lhs[...], grad_low), (lhs2, stream_low))):
        for i in range(WIDTH // tile):
            r = dot(left, right[:, i * tile : (i + 1) * tile])
            cols = slice(j * WIDTH + i * tile, j * WIDTH + (i + 1) * tile)
            for z in range(4):
                give(z, r[z * 128 : (z + 1) * 128] + got[z, :, cols].astype(F32), cols)
    cols = slice(2 * WIDTH, RIGHT)
    for z in range(4):
        rows = pl.ds(pl.multiple_of((z * 2 + core) * 128, 128), 128)
        total = gain_col[rows, :] + got[z, :, cols].astype(F32)
        for d, out in enumerate(outs):
            square[:, :GAIN] = total
            part = square[pl.ds(pl.multiple_of((place[2] ^ d) * 32, 32), 32), :]
            out[z, :, cols] = part[:, :GAIN].astype(out.dtype)


def table_kernel(place, m0, m1, m2, m3, give_o, keep_o, square):
    core = place[1]
    for k in range(BOOKS):
        lanes = slice(k * RANK, (k + 1) * RANK)
        lowrank = jnp.concatenate([m[AUDIO:, lanes] for m in (m0, m1, m2, m3)], axis=0)
        marks = jnp.concatenate([m[:AUDIO, WIDTH:] for m in (m0, m1, m2, m3)], axis=0).astype(F32)
        high = marks[:, k : k + 1].astype(I32)
        low = marks[:, BOOKS + k : BOOKS + k + 1].astype(I32)
        at = jnp.where(high % 4 == place[2], (high // 4) * 64 + low, -1)
        spread = ones_where(at == iota((4 * AUDIO, 512), 1))
        square[k * 512 : (k + 1) * 512, :] = dot(spread, lowrank, TN)
    for half, out in ((1 - core, give_o), (core, keep_o)):
        for z in range(4):
            for r in range(16):
                at = (z * 2 + half) * 64 + r
                block = [square[pl.ds(at + y * 16, 8, stride=512), :] for y in range(4)]
                out[z, :, r * 128 : (r + 1) * 128] = jnp.concatenate(block, axis=0).astype(out.dtype)


def win_kernel(place, p0, p1, p2, p3, chosen, give_o, keep_o, order, rows):
    core = place[1]
    for dy, p in enumerate((p0, p1, p2, p3)):
        for dx in range(4):
            device = (place[2] ^ dx) * 4 + (place[3] ^ dy)
            here = (dy * 4 + dx) * AUDIO
            source = pl.ds(pl.multiple_of(device * AUDIO, AUDIO), AUDIO)
            order[here : here + AUDIO, :] = chosen[source, :]
            rows[here : here + AUDIO, :] = p[dx * AUDIO : (dx + 1) * AUDIO, :]
    features = jnp.transpose(order[...])
    for half, out in ((1 - core, give_o), (core, keep_o)):
        for z in range(4):
            cols = pl.ds(pl.multiple_of((z * 2 + half) * 128, 128), 128)
            out[z] = dot(features, rows[:, cols]).astype(out.dtype)


def win_meet_kernel(place, keep, got, o0, o1, o2, o3):
    for d, out in enumerate((o0, o1, o2, o3)):
        z = place[0] ^ d
        out[...] = (keep[z] + got[z].astype(F32)).astype(out.dtype)


def left_kernel(place, l0, g1, g2, g3, o0, o1, o2, o3, total):
    total[...] = l0[...] + g1[...].astype(F32) + g2[...].astype(F32) + g3[...].astype(F32)
    for d, out in enumerate((o0, o1, o2, o3)):
        rows = pl.ds(pl.multiple_of((place[2] ^ d) * 32, 32), 32)
        out[...] = total[rows, :].astype(out.dtype)


def right_kernel(place, r0, g1, g2, g3, keep, got, o0, o1, o2, o3):
    for d, out in enumerate((o0, o1, o2, o3)):
        z = place[0] ^ d
        total = r0[z] + g1[z].astype(F32) + g2[z].astype(F32) + g3[z].astype(F32)
        out[:, :RIGHT] = total.astype(out.dtype)
        out[:, RIGHT:] = (keep[z] + got[z].astype(F32)).astype(out.dtype)


def meet_kernel(place, l0, l1, l2, l3, r0, r1, r2, r3, o0, o1, o2, o3, left, right):
    left[...] = l0[...] + l1[...].astype(F32) + l2[...].astype(F32) + l3[...].astype(F32)
    right[...] = r0[...] + r1[...].astype(F32) + r2[...].astype(F32) + r3[...].astype(F32)
    half = LEFT // 2
    for d, out in enumerate((o0, o1, o2, o3)):
        rows = pl.ds(pl.multiple_of((place[3] ^ d) * 8, 8), 8)
        out[:, :half] = jnp.concatenate([left[rows, :half], left[rows, half:]], axis=0).astype(out.dtype)
        block = right[rows, RIGHT:]
        block = jnp.concatenate([block, jnp.zeros((8, RIGHT - TABLE), F32)], axis=1)
        out[:, half:] = jnp.concatenate([right[rows, :RIGHT], block], axis=0).astype(out.dtype)


def last_kernel(a, b, c, d, qkv_o, wout_o, b_o, gain_o, table_o):
    total = a[...] + b[...].astype(F32) + c[...].astype(F32) + d[...].astype(F32)
    half = LEFT // 2
    qkv_o[:, :half] = total[:8, :half]
    qkv_o[:, half:] = total[8:, :half]
    wout_o[...] = total[:8, half : half + WIDTH]
    b_o[:, 0, :] = total[:8, half + WIDTH : half + 2 * WIDTH]
    gain_o[...] = total[:8, half + 2 * WIDTH :]
    for r in range(16):
        table_o[:, r, :] = total[8:, half + r * 128 : half + (r + 1) * 128]


def temporal_kernel(place, keeps, goes, p0, p1, p2, p3, w_in, out, grad):
    for dy, p in enumerate((p0, p1, p2, p3)):
        grad[dy * 192 : (dy + 1) * 192, :] = dot(p[...], w_in[...], NT).astype(BF16)
    slots = iota((AUDIO, BLOCK), 0)

    def of_device(x, y):
        at = ((y ^ place[3]) * 4 + (x ^ place[2])) * AUDIO
        return grad[pl.ds(pl.multiple_of(at, AUDIO), AUDIO), :]

    for b in range(TPS):
        x, y = b // 4, b % 4
        mine = dot(ones_where(keeps[b : b + 1] == slots), of_device(x, y), TN)
        theirs = dot(ones_where(goes[b : b + 1] == slots), of_device(x ^ 2, y), TN)
        out[b * BLOCK : (b + 1) * BLOCK, :] = (mine + theirs).astype(BF16)


def swap(x, axis, n, d):
    return lax.ppermute(x, axis, [(i, i ^ d) for i in range(n)])


def swaps(parts, axis):
    return (parts[0],) + tuple(swap(parts[d], axis, 4, d) for d in (1, 2, 3))


def after(x, *others):
    return lax.optimization_barrier((x,) + others)[0]


def to_all(x, axes):
    return lax.all_to_all(x, axes, 0, 0, tiled=True)


def local(
    temporal, w_in, audio_mask, counts, codes, cotangent, norm_gain, w_qkv, w_out, adapter_a, adapter_b
):
    x_at, y_at = lax.axis_index("x"), lax.axis_index("y")
    z_at, c_at = lax.axis_index("z"), lax.axis_index("c")
    place = jnp.stack([z_at, c_at, x_at, y_at, x_at * 4 + y_at]).astype(I32)
    mask = audio_mask.reshape(TPS, BLOCK)
    cot_rows = cotangent.reshape(BLOCK * BOOKS, WIDTH)
    gain = norm_gain.reshape(1, WIDTH)

    group = 4 * AUDIO
    *parts, chosen, keeps, goes, code_leave = call(
        project_kernel, "project",
        (shaped(group, WIDTH, dtype=F32),) + (shaped(group, WIDTH),) * 3
        + (shaped(TPS * AUDIO, 256), shaped(TPS, BLOCK, dtype=I32), shaped(TPS, BLOCK, dtype=I32),
           shaped(EXTRA, BOOKS, dtype=I32)),
        (place, mask, temporal, w_in, codes), scalars=1, scratch=[pltpu.VMEM((group, 256), BF16)],
    )
    code_come = swap(code_leave, "x", 4, 2)
    near = [swap(parts[d], "y", 4, d) for d in (1, 3)]
    cot_leave = call(
        leave_kernel, "leave", shaped(EXTRA * BOOKS, WIDTH), (after(place, chosen), mask, cot_rows), scalars=1,
    )
    far, cot_leave, code_come, *near = lax.optimization_barrier((parts[2], cot_leave, code_come, *near))
    parts = (parts[0], near[0], swap(far, "y", 4, 2), near[1])
    cot_come = swap(cot_leave, "x", 4, 2)
    tokens, low, embedded = call(
        embed_kernel, "embed",
        (shaped(AUDIO, BOOKS, dtype=I32), shaped(ROWS, RANK), shaped(ROWS, WIDTH, dtype=F32)),
        (after(place, code_come), mask, codes, code_come, adapter_a, adapter_b), scalars=1,
    )
    parts = call(
        project_meet_kernel, "project_meet", (shaped(AUDIO, WIDTH, dtype=F32),) + (shaped(AUDIO, WIDTH),) * 3,
        (after(place, low),) + parts, scalars=1, scratch=[pltpu.VMEM((group, WIDTH), F32)],
    )
    parts = swaps(parts, "x")
    cot, weights, grad_low, grad_mixed = call(
        upstream_kernel, "upstream",
        (shaped(ROWS, WIDTH), shaped(ROWS, 128, dtype=F32), shaped(ROWS, WIDTH), shaped(ROWS, WIDTH)),
        (after(place, parts[0]), mask, cot_rows, cot_come, w_out), scalars=1,
    )
    normed, mixed, packed, stream, inv, probs = call(
        forward_kernel, "forward",
        (shaped(ROWS, WIDTH), shaped(ROWS, WIDTH), shaped(ROWS, 3 * WIDTH),
         shaped(ROWS, WIDTH, dtype=F32), shaped(ROWS, 128, dtype=F32),
         shaped(HEADS // 2 * ROWS, 256, dtype=F32)),
        (*parts, embedded, after(gain, grad_mixed), w_qkv), limit=16,
    )
    grad_packed, give = call(
        backward_give_kernel, "backward", (shaped(ROWS, 3 * WIDTH), shaped(4, 128, LEFT)),
        (place, packed, probs, grad_mixed, normed), scalars=1,
        scratch=[pltpu.VMEM((512, ROWS), BF16)], limit=12,
    )
    got_left = swap(give, "c", 2, 1)
    message, stream_low, gain_col, give_late = call(
        norm_give_kernel, "norm",
        (shaped(2 * AUDIO, WIDTH + RANK), shaped(ROWS, WIDTH), shaped(WIDTH, 128, dtype=F32), shaped(4, 128, RIGHT)),
        (place, grad_packed, w_qkv, stream, inv, cot, weights, gain, adapter_b, tokens, mixed, grad_low, low),
        scalars=1, scratch=[pltpu.VMEM((ROWS, WIDTH), F32), pltpu.VMEM((512, ROWS), BF16)], limit=16,
    )
    got_late = swap(give_late, "c", 2, 1)
    messages = swaps((message,) * 4, "x")
    lefts = call(
        keep_left_kernel, "keep_left",
        (shaped(128, LEFT, dtype=F32),) + (shaped(128, LEFT),) * 3,
        (after(place, message), normed, grad_packed, got_left), scalars=1,
        scratch=[pltpu.VMEM((512, ROWS), BF16)],
    )
    rights = call(
        keep_right_kernel, "keep_right",
        (shaped(4, 32, RIGHT, dtype=F32),) + (shaped(4, 32, RIGHT),) * 3,
        (after(place, lefts[1]), mixed, grad_low, low, stream_low, gain_col, got_late),
        scalars=1, scratch=[pltpu.VMEM((512, ROWS), BF16), pltpu.VMEM((128, 512), F32)],
    )
    give_table, keep_table = call(
        table_kernel, "table",
        (shaped(4, 32, TABLE), shaped(4, 32, TABLE, dtype=F32)),
        (after(place, rights[1]),) + messages, scalars=1, scratch=[pltpu.VMEM((BOOKS * 512, 128), F32)],
    )
    got_table = swap(give_table, "c", 2, 1)
    near = [swap(lefts[d], "z", 4, d) for d in (1, 3)] + [swap(rights[d], "x", 4, d) for d in (1, 3)]
    piece = jnp.concatenate([m[:AUDIO, :WIDTH] for m in messages], axis=0)
    far_left, far_right, piece, got_table, *near = lax.optimization_barrier(
        (lefts[2], rights[2], piece, got_table, *near)
    )
    far_left, far_right = swap(far_left, "z", 4, 2), swap(far_right, "x", 4, 2)
    lefts = (lefts[0], near[0], far_left, near[1])
    rights = (rights[0], near[2], far_right, near[3])
    pieces = swaps((piece,) * 4, "y")
    rights = call(
        right_kernel, "right", (shaped(32, RIGHT + TABLE, dtype=F32),) + (shaped(32, RIGHT + TABLE),) * 3,
        (place,) + rights + (keep_table, got_table), scalars=1,
    )
    rights = swaps(rights, "z")
    lefts = call(
        left_kernel, "left", (shaped(32, LEFT, dtype=F32),) + (shaped(32, LEFT),) * 3,
        (place,) + lefts, scalars=1, scratch=[pltpu.VMEM((128, LEFT), F32)],
    )
    lefts = swaps(lefts, "x")
    give_win, keep_win = call(
        win_kernel, "win", (shaped(4, 256, 128), shaped(4, 256, 128, dtype=F32)),
        (place,) + pieces + (chosen,), scalars=1,
        scratch=[pltpu.VMEM((TPS * AUDIO, 256), BF16), pltpu.VMEM((TPS * AUDIO, WIDTH), BF16)],
    )
    got_win = swap(give_win, "c", 2, 1)
    wins = call(
        win_meet_kernel, "win_meet", (shaped(256, 128, dtype=F32),) + (shaped(256, 128),) * 3,
        (place, keep_win, got_win), scalars=1,
    )
    wins = swaps(wins, "z")
    columns = LEFT // 2 + RIGHT
    meets = call(
        meet_kernel, "meet", (shaped(16, columns, dtype=F32),) + (shaped(16, columns),) * 3,
        (place,) + lefts + rights, scalars=1,
        scratch=[pltpu.VMEM((32, LEFT), F32), pltpu.VMEM((32, RIGHT + TABLE), F32)],
    )
    grad_temporal = call(
        temporal_kernel, "temporal", shaped(TPS * BLOCK, 256),
        (after(place, meets[1]), keeps, goes) + pieces + (w_in,), scalars=1,
        scratch=[pltpu.VMEM((TPS * AUDIO, 256), BF16)],
    )
    meets = swaps(meets, "y")
    grad_win = wins[0] + wins[1].astype(F32) + wins[2].astype(F32) + wins[3].astype(F32)
    grad_wqkv, grad_wout, grad_b, grad_gain, grad_a = call(
        last_kernel, "last",
        (shaped(8, LEFT, dtype=F32), shaped(8, WIDTH, dtype=F32), shaped(BOOKS, 1, WIDTH, dtype=F32),
         shaped(8, GAIN, dtype=F32), shaped(BOOKS, 16, RANK, dtype=F32)),
        meets,
    )
    return (
        grad_temporal,
        grad_win,
        grad_gain[:, 0],
        grad_wqkv,
        grad_wout,
        grad_a,
        grad_b,
    )


def solution(mesh):
    grid = Mesh(mesh.devices.reshape(4, 2, 4, 4), ("z", "c", "x", "y"))
    seq, tp = ("z", "c"), ("x", "y")
    every = seq + tp
    placed = (
        P(seq, tp),
        P(tp, None),
        P(seq),
        P(),
        P(every, None),
        P(every, None, None),
        P(),
        P(),
        P(),
        P(),
        P(),
    )
    return jax.shard_map(
        local,
        mesh=grid,
        in_specs=placed,
        out_specs=(
            P(seq, tp),
            P(tp, seq),
            P(every),
            P(every, None),
            P(every, None),
            P(None, every, None),
            P(None, every, None),
        ),
        check_vma=False,
    )
```

```python
import math

import jax
import jax.numpy as jnp
from jax import lax
from jax.experimental import pallas as pl
from jax.experimental.pallas import tpu as pltpu
from jax.sharding import Mesh, PartitionSpec as P

HEADS = 16
AUDIO = 48
EXTRA = 40
BLOCK = 96
BOOKS = 8
RANK = 128
GROUP = 16
GROUPS = AUDIO // GROUP
ROWS = AUDIO * BOOKS
SPAN = GROUP * BOOKS
TPS = 16
WIDTH = 1024
VOCAB = 2048
LEFT = 3 * WIDTH
GAIN = 128
RIGHT = 5 * WIDTH + GAIN - LEFT
TABLE = VOCAB
F32 = jnp.float32
BF16 = jnp.bfloat16
I32 = jnp.int32
NT = (((1,), (1,)), ((), ()))
TN = (((0,), (0,)), ((), ()))
MIB = 1024 * 1024


def dot(a, b, dims=None):
    if dims is None:
        return jnp.dot(a, b, preferred_element_type=F32)
    return lax.dot_general(a, b, dims, preferred_element_type=F32)


def iota(shape, dim):
    return lax.broadcasted_iota(I32, shape, dim)


def ones_where(cond):
    return jnp.where(cond, 1.0, 0.0).astype(BF16)


def shaped(*shape, dtype=BF16):
    return jax.ShapeDtypeStruct(shape, dtype)


def call(kernel, name, out, args, scalars=0, scratch=(), limit=12):
    vmem = pl.BlockSpec(memory_space=pltpu.VMEM)
    smem = pl.BlockSpec(memory_space=pltpu.SMEM)
    return pl.pallas_call(
        kernel,
        out_shape=out,
        in_specs=[smem] * scalars + [vmem] * (len(args) - scalars),
        out_specs=jax.tree.map(lambda _: vmem, out),
        scratch_shapes=list(scratch),
        compiler_params=pltpu.CompilerParams(vmem_limit_bytes=limit * MIB),
        cost_estimate=pl.CostEstimate(flops=0, bytes_accessed=0, transcendentals=0),
        name=name,
    )(*args)


def ranks(mask_ref):
    mask = mask_ref[...].astype(F32)
    before = ones_where(iota((BLOCK, BLOCK), 0) < iota((BLOCK, BLOCK), 1))
    rank = dot(mask.astype(BF16), before)
    return mask > 0, rank, jnp.sum(mask, axis=1, keepdims=True)


def own_row(a, column):
    a = jnp.broadcast_to(a, (TPS, a.shape[1]))
    return jnp.sum(jnp.where(iota(a.shape, 0) == column, a, 0.0), axis=0, keepdims=True)


def each_book(row):
    spread = ones_where(iota((BLOCK, BLOCK * BOOKS), 1) // BOOKS == iota((BLOCK, BLOCK * BOOKS), 0))
    wide = dot(jnp.broadcast_to(row, (8, BLOCK)).astype(BF16), spread)
    return wide[:1].astype(I32)


def select_codes(chosen, codes):
    high = dot(chosen, (codes >> 6).astype(F32).astype(BF16))
    low = dot(chosen, (codes & 63).astype(F32).astype(BF16))
    return high.astype(I32) * 64 + low.astype(I32)


def project_kernel(
    place, mask, temporal, w_in, codes, o0, o1, o2, o3, chosen, keeps_o, goes_o, code_o, rows
):
    audio, rank, count = ranks(mask)
    leaves = own_row(jnp.where(audio & (rank >= AUDIO), rank - AUDIO, -1.0), place[4])
    code_o[...] = select_codes(ones_where(leaves.astype(I32) == iota((EXTRA, BLOCK), 0)), codes[...])
    keeps = jnp.where(audio & (rank < AUDIO), rank, -1.0).astype(I32)
    goes = jnp.where(audio & (rank >= AUDIO), rank + AUDIO - count, -1.0).astype(I32)
    keeps_o[...] = keeps
    goes_o[...] = goes
    slots = iota((AUDIO, BLOCK), 0)
    for b in range(TPS):
        o = b ^ 8
        mine = dot(ones_where(keeps[b : b + 1] == slots), temporal[b * BLOCK : (b + 1) * BLOCK, :])
        theirs = dot(ones_where(goes[o : o + 1] == slots), temporal[o * BLOCK : (o + 1) * BLOCK, :])
        chosen[b * AUDIO : (b + 1) * AUDIO, :] = (mine + theirs).astype(BF16)
    for d, out in enumerate((o0, o1, o2, o3)):
        for x in range(4):
            source = pl.ds(pl.multiple_of((x * 4 + (place[3] ^ d)) * AUDIO, AUDIO), AUDIO)
            rows[x * AUDIO : (x + 1) * AUDIO, :] = chosen[source, :]
        out[...] = dot(rows[...], w_in[...]).astype(out.dtype)


def project_meet_kernel(place, p0, p1, p2, p3, o0, o1, o2, o3, total):
    total[...] = p0[...] + p1[...].astype(F32) + p2[...].astype(F32) + p3[...].astype(F32)
    for d, out in enumerate((o0, o1, o2, o3)):
        rows = pl.ds(pl.multiple_of((place[2] ^ d) * AUDIO, AUDIO), AUDIO)
        out[...] = total[rows, :].astype(out.dtype)


def leave_kernel(place, mask, cot, cot_o):
    audio, rank, _ = ranks(mask)
    row = own_row(jnp.where(audio & (rank >= AUDIO), rank - AUDIO, -1.0), place[4])
    wide = each_book(row)
    key = jnp.where(wide >= 0, wide * BOOKS + iota(wide.shape, 1) % BOOKS, -1)
    spread = ones_where(key == iota((EXTRA * BOOKS, BLOCK * BOOKS), 0))
    for i in range(2):
        cols = slice(i * 512, (i + 1) * 512)
        cot_o[:, cols] = dot(spread, cot[:, cols]).astype(BF16)


def embed_kernel(place, mask, codes, codes_come, table, adapter_b, tokens_o, low_o, embedded_o):
    audio, rank, count = ranks(mask)
    row = own_row(jnp.where(audio & (rank < AUDIO), rank, -1.0), place[4]).astype(I32)
    have = own_row(count, place[4]).astype(I32)
    comes = jnp.broadcast_to(have, (1, EXTRA)) + iota((1, EXTRA), 1)
    tokens = select_codes(ones_where(row == iota((AUDIO, BLOCK), 0)), codes[...])
    tokens = tokens + select_codes(ones_where(comes == iota((AUDIO, EXTRA), 0)), codes_come[...])
    tokens_o[...] = tokens
    vocab = iota((AUDIO, VOCAB), 1)
    for k in range(BOOKS):
        rows = slice(k * AUDIO, (k + 1) * AUDIO)
        low = dot(ones_where(tokens[:, k : k + 1] == vocab), table[k]).astype(BF16)
        low_o[rows, :] = low
        embedded_o[rows, :] = dot(low, adapter_b[k])


def upstream_kernel(place, mask, cot, cot_come, w_out, cot_o, weights_o, grad_low_o, grad_mixed_o):
    audio, rank, count = ranks(mask)
    row = own_row(jnp.where(audio & (rank < AUDIO), rank, -1.0), place[4])
    have = own_row(count, place[4])
    slot = iota((ROWS, 128), 0)
    slot = (slot // SPAN) * GROUP + slot % GROUP
    weights = jnp.where(slot < have.astype(I32), AUDIO / have, AUDIO / (BLOCK - have))
    weights_o[...] = weights

    def target(at, book):
        return jnp.where((at >= 0) & (at < AUDIO), (at // GROUP) * SPAN + book * GROUP + at % GROUP, -1)

    wide = each_book(row)
    stays = ones_where(target(wide, iota(wide.shape, 1) % BOOKS) == iota((ROWS, BLOCK * BOOKS), 0))
    index = iota((1, EXTRA * BOOKS), 1)
    come = jnp.broadcast_to(have.astype(I32), index.shape) + index // BOOKS
    comes = ones_where(target(come, index % BOOKS) == iota((ROWS, EXTRA * BOOKS), 0))
    for i in range(2):
        cols = slice(i * 512, (i + 1) * 512)
        here = dot(stays, cot[:, cols]) + dot(comes, cot_come[:, cols])
        cot_o[:, cols] = here.astype(BF16)
        grad_low_o[:, cols] = (here * weights[:, :1]).astype(BF16)
    for i in range(4):
        cols = slice(i * 256, (i + 1) * 256)
        grad_mixed_o[:, cols] = dot(grad_low_o[...], w_out[cols, :], NT).astype(BF16)


def split(a):
    first = iota((SPAN, 128), 1) < 64
    zero = jnp.zeros_like(a)
    return jnp.concatenate([jnp.where(first, a, zero), jnp.where(first, zero, a)], axis=0)


def pick(a):
    return jnp.where(iota((SPAN, 128), 1) < 64, a[:SPAN], a[SPAN:])


def pair_columns(part, p):
    return pl.ds(pl.multiple_of(part * WIDTH + p * 128, 128), 128)


def pair_probs(p, g):
    return pl.ds(pl.multiple_of((p * GROUPS + g) * SPAN, SPAN), SPAN)


SCALE = 1.0 / math.sqrt(64)


def forward_kernel(
    p0, p1, p2, p3, embedded, gain, w_qkv, normed_o, mixed_o, packed_o, stream_o, inv_o, probs_o
):
    for g in range(GROUPS):
        frames = pl.ds(g * GROUP, GROUP)
        proj = p0[frames, :] + p1[frames, :].astype(F32) + p2[frames, :].astype(F32) + p3[frames, :].astype(F32)
        proj = proj.astype(BF16).astype(F32)
        for k in range(BOOKS):
            rows = pl.ds(g * SPAN + k * GROUP, GROUP)
            x = proj + embedded[pl.ds(k * AUDIO + g * GROUP, GROUP), :]
            stream_o[rows, :] = x
            a = lax.rsqrt(jnp.mean(x * x, axis=-1, keepdims=True) + 1e-05)
            inv_o[rows, :] = jnp.broadcast_to(a, (GROUP, 128))
            normed_o[rows, :] = (x * a * gain[...]).astype(BF16)

    tile = 512

    @pl.loop(0, 3 * WIDTH // tile)
    def _(i):
        cols = pl.ds(pl.multiple_of(i * tile, tile), tile)
        packed_o[:, cols] = dot(normed_o[...], w_qkv[:, cols]).astype(BF16)

    key_row = iota((SPAN, 2 * SPAN), 0)
    query_row = iota((SPAN, 2 * SPAN), 1) % SPAN
    allowed = (key_row % GROUP == query_row % GROUP) & (key_row // GROUP <= query_row // GROUP)

    @pl.loop(0, HEADS // 16)
    def _(half):
        for p, g in ((half * 8 + i, g) for i in range(8) for g in range(GROUPS)):
            rows = pl.ds(g * SPAN, SPAN)
            query = split(packed_o[rows, pair_columns(0, p)])
            keys = packed_o[rows, pair_columns(1, p)]
            values = packed_o[rows, pair_columns(2, p)]
            scores = jnp.where(allowed, dot(keys, query, NT) * SCALE, -1e30)
            top = jnp.max(scores, axis=0, keepdims=True)
            e = jnp.exp(scores - top)
            probs = e * (1.0 / jnp.sum(e, axis=0, keepdims=True))
            probs_o[pair_probs(p, g), :] = probs
            mixed = pick(dot(probs.astype(BF16), values, TN))
            mixed_o[rows, pair_columns(0, p)] = mixed.astype(BF16)


def backward_kernel(packed, probs_in, grad_mixed, packed_grad_o):
    @pl.loop(0, HEADS // 16)
    def _(half):
        for p, g in ((half * 8 + i, g) for i in range(8) for g in range(GROUPS)):
            rows = pl.ds(g * SPAN, SPAN)
            query = split(packed[rows, pair_columns(0, p)])
            keys = packed[rows, pair_columns(1, p)]
            values = packed[rows, pair_columns(2, p)]
            gm = split(grad_mixed[rows, pair_columns(0, p)])
            probs = probs_in[pair_probs(p, g), :]
            grad_probs = dot(values, gm, NT)
            packed_grad_o[rows, pair_columns(2, p)] = dot(probs.astype(BF16), gm).astype(BF16)
            inner = jnp.sum(probs * grad_probs, axis=0, keepdims=True)
            grad_scores = (probs * (grad_probs - inner) * SCALE).astype(BF16)
            grad_query = pick(dot(grad_scores, keys, TN))
            packed_grad_o[rows, pair_columns(0, p)] = grad_query.astype(BF16)
            packed_grad_o[rows, pair_columns(1, p)] = dot(grad_scores, query).astype(BF16)


def norm_kernel(
    packed_grad, w_qkv, stream, inv, cot, weights, gain, adapter_b,
    tokens, message_o, stream_low_o, gain_o, grad_normed,
):
    tile = 256

    @pl.loop(0, WIDTH // tile)
    def _(i):
        cols = pl.ds(pl.multiple_of(i * tile, tile), tile)
        grad_normed[:, cols] = dot(packed_grad[...], w_qkv[cols, :], NT)

    gain_sum = jnp.zeros((GROUP, WIDTH), F32)
    for g in range(GROUPS):
        total = jnp.zeros((GROUP, WIDTH), F32)
        for k in range(BOOKS):
            rows = pl.ds(g * SPAN + k * GROUP, GROUP)
            x = stream[rows, :]
            a = inv[rows, :][:, :1]
            gn = grad_normed[rows, :]
            gain_sum = gain_sum + gn * (x * a)
            scaled = gn * gain[...]
            mean = jnp.mean(scaled * x, axis=-1, keepdims=True)
            grad_out = cot[rows, :].astype(F32) * weights[rows, :][:, :1]
            gs = grad_out + a * (scaled - x * (a * a * mean))
            total = total + gs
            stream_low_o[pl.ds(k * AUDIO + g * GROUP, GROUP), :] = gs.astype(BF16)
        message_o[pl.ds(g * GROUP, GROUP), :WIDTH] = total.astype(BF16)
    gain_row = jnp.sum(gain_sum, axis=0, keepdims=True)
    for i in range(WIDTH // 128):
        piece = jnp.broadcast_to(gain_row[:, i * 128 : (i + 1) * 128], (128, 128))
        gain_o[i * 128 : (i + 1) * 128, :] = jnp.transpose(piece)
    for k in range(BOOKS):
        rows = pl.ds(k * AUDIO, AUDIO)
        lowrank = dot(stream_low_o[rows, :], adapter_b[k], NT).astype(BF16)
        message_o[AUDIO:, k * RANK : (k + 1) * RANK] = lowrank
    marks = jnp.zeros((AUDIO, RANK), F32)
    for k in range(BOOKS):
        token = jnp.broadcast_to(tokens[:, k : k + 1], (AUDIO, RANK))
        lane = iota((AUDIO, RANK), 1)
        marks = jnp.where(lane == k, (token >> 6).astype(F32), marks)
        marks = jnp.where(lane == BOOKS + k, (token & 63).astype(F32), marks)
    message_o[:AUDIO, WIDTH:] = marks.astype(BF16)
    message_o[AUDIO:, WIDTH:] = jnp.zeros((AUDIO, RANK), BF16)


def columns_of(a, core, order):
    return [jnp.transpose(a[:, pl.ds(pl.multiple_of((z * 2 + core) * 128, 128), 128)]) for z in order]


def give_kernel(place, normed, packed_grad, out, lhs):
    for i, block in enumerate(columns_of(normed, 1 - place[1], range(4))):
        lhs[i * 128 : (i + 1) * 128, :] = block
    tile = 512
    for i in range(LEFT // tile):
        cols = slice(i * tile, (i + 1) * tile)
        r = dot(lhs[...], packed_grad[:, cols]).astype(BF16)
        for z in range(4):
            out[z, :, cols] = r[z * 128 : (z + 1) * 128]


def backward_give_kernel(place, packed, probs_in, grad_mixed, normed, packed_grad_o, give_o, lhs):
    backward_kernel(packed, probs_in, grad_mixed, packed_grad_o)
    give_kernel(place, normed, packed_grad_o, give_o, lhs)


def norm_give_kernel(
    place, packed_grad, w_qkv, stream, inv, cot, weights, gain, adapter_b, tokens, mixed, grad_low, low,
    message_o, stream_low_o, gain_o, give_o, grad_normed, lhs,
):
    norm_kernel(
        packed_grad, w_qkv, stream, inv, cot, weights, gain, adapter_b, tokens,
        message_o, stream_low_o, gain_o, grad_normed,
    )
    give_late_kernel(place, mixed, grad_low, low, stream_low_o, gain_o, give_o, lhs)


def keep_left_kernel(place, normed, packed_grad, got, l0, l1, l2, l3, lhs):
    outs = (l0, l1, l2, l3)
    order = [place[0] ^ d for d in range(4)]
    for i, block in enumerate(columns_of(normed, place[1], order)):
        lhs[i * 128 : (i + 1) * 128, :] = block
    tile = 512
    for i in range(LEFT // tile):
        cols = slice(i * tile, (i + 1) * tile)
        r = dot(lhs[...], packed_grad[:, cols])
        for d in range(4):
            total = r[d * 128 : (d + 1) * 128] + got[order[d], :, cols].astype(F32)
            outs[d][:, cols] = total.astype(outs[d].dtype)


def rank_rows(low, rank, book):
    chosen = dot(ones_where(rank == iota((512, RANK), 1)), low[...], NT)
    return jnp.where(iota((512, ROWS), 1) // AUDIO == book, chosen, 0.0).astype(BF16)


def give_late_kernel(place, mixed, grad_low, low, stream_low, gain_col, out, lhs):
    other = 1 - place[1]
    for i, block in enumerate(columns_of(mixed, other, range(4))):
        lhs[i * 128 : (i + 1) * 128, :] = block
    row = iota((512, 1), 0)
    lhs2 = rank_rows(low, (row // 128) * 32 + other * 16 + (row % 128) // 8, row % 8)
    tile = 512
    for j, (left, right) in enumerate(((lhs[...], grad_low), (lhs2, stream_low))):
        for i in range(WIDTH // tile):
            r = dot(left, right[:, i * tile : (i + 1) * tile]).astype(BF16)
            at = j * WIDTH + i * tile
            for z in range(4):
                out[z, :, at : at + tile] = r[z * 128 : (z + 1) * 128]
    for z in range(4):
        rows = pl.ds(pl.multiple_of((z * 2 + other) * 128, 128), 128)
        out[z, :, 2 * WIDTH :] = gain_col[rows, :].astype(BF16)


def keep_right_kernel(place, mixed, grad_low, low, stream_low, gain_col, got, r0, r1, r2, r3, lhs, square):
    outs = (r0, r1, r2, r3)
    core = place[1]
    for z, block in enumerate(columns_of(mixed, core, range(4))):
        lhs[z * 128 : (z + 1) * 128, :] = block
    row = iota((512, 1), 0)
    lhs2 = rank_rows(low, (row // 128) * 32 + core * 16 + (row % 128) // 8, row % 8)

    def give(z, total, cols):
        square[...] = total
        for d, out in enumerate(outs):
            rows = pl.ds(pl.multiple_of((place[2] ^ d) * 32, 32), 32)
            out[z, :, cols] = square[rows, :].astype(out.dtype)

    tile = 512
    for j, (left, right) in enumerate(((lhs[...], grad_low), (lhs2, stream_low))):
        for i in range(WIDTH // tile):
            r = dot(left, right[:, i * tile : (i + 1) * tile])
            cols = slice(j * WIDTH + i * tile, j * WIDTH + (i + 1) * tile)
            for z in range(4):
                give(z, r[z * 128 : (z + 1) * 128] + got[z, :, cols].astype(F32), cols)
    cols = slice(2 * WIDTH, RIGHT)
    for z in range(4):
        rows = pl.ds(pl.multiple_of((z * 2 + core) * 128, 128), 128)
        total = gain_col[rows, :] + got[z, :, cols].astype(F32)
        for d, out in enumerate(outs):
            square[:, :GAIN] = total
            part = square[pl.ds(pl.multiple_of((place[2] ^ d) * 32, 32), 32), :]
            out[z, :, cols] = part[:, :GAIN].astype(out.dtype)


def table_kernel(place, m0, m1, m2, m3, give_o, keep_o, square):
    core = place[1]
    for k in range(BOOKS):
        lanes = slice(k * RANK, (k + 1) * RANK)
        lowrank = jnp.concatenate([m[AUDIO:, lanes] for m in (m0, m1, m2, m3)], axis=0)
        marks = jnp.concatenate([m[:AUDIO, WIDTH:] for m in (m0, m1, m2, m3)], axis=0).astype(F32)
        high = marks[:, k : k + 1].astype(I32)
        low = marks[:, BOOKS + k : BOOKS + k + 1].astype(I32)
        at = jnp.where(high % 4 == place[2], (high // 4) * 64 + low, -1)
        spread = ones_where(at == iota((4 * AUDIO, 512), 1))
        square[k * 512 : (k + 1) * 512, :] = dot(spread, lowrank, TN)
    for half, out in ((1 - core, give_o), (core, keep_o)):
        for z in range(4):
            for r in range(16):
                at = (z * 2 + half) * 64 + r
                block = [square[pl.ds(at + y * 16, 8, stride=512), :] for y in range(4)]
                out[z, :, r * 128 : (r + 1) * 128] = jnp.concatenate(block, axis=0).astype(out.dtype)


def win_kernel(place, p0, p1, p2, p3, chosen, give_o, keep_o, order, rows):
    core = place[1]
    for dy, p in enumerate((p0, p1, p2, p3)):
        for dx in range(4):
            device = (place[2] ^ dx) * 4 + (place[3] ^ dy)
            here = (dy * 4 + dx) * AUDIO
            source = pl.ds(pl.multiple_of(device * AUDIO, AUDIO), AUDIO)
            order[here : here + AUDIO, :] = chosen[source, :]
            rows[here : here + AUDIO, :] = p[dx * AUDIO : (dx + 1) * AUDIO, :]
    features = jnp.transpose(order[...])
    for half, out in ((1 - core, give_o), (core, keep_o)):
        for z in range(4):
            cols = pl.ds(pl.multiple_of((z * 2 + half) * 128, 128), 128)
            out[z] = dot(features, rows[:, cols]).astype(out.dtype)


def win_meet_kernel(place, keep, got, o0, o1, o2, o3):
    for d, out in enumerate((o0, o1, o2, o3)):
        z = place[0] ^ d
        out[...] = (keep[z] + got[z].astype(F32)).astype(out.dtype)


def left_kernel(place, l0, g1, g2, g3, o0, o1, o2, o3, total):
    total[...] = l0[...] + g1[...].astype(F32) + g2[...].astype(F32) + g3[...].astype(F32)
    for d, out in enumerate((o0, o1, o2, o3)):
        rows = pl.ds(pl.multiple_of((place[2] ^ d) * 32, 32), 32)
        out[...] = total[rows, :].astype(out.dtype)


def right_kernel(place, r0, g1, g2, g3, keep, got, o0, o1, o2, o3):
    for d, out in enumerate((o0, o1, o2, o3)):
        z = place[0] ^ d
        total = r0[z] + g1[z].astype(F32) + g2[z].astype(F32) + g3[z].astype(F32)
        out[:, :RIGHT] = total.astype(out.dtype)
        out[:, RIGHT:] = (keep[z] + got[z].astype(F32)).astype(out.dtype)


def meet_kernel(place, l0, l1, l2, l3, r0, r1, r2, r3, o0, o1, o2, o3, left, right):
    left[...] = l0[...] + l1[...].astype(F32) + l2[...].astype(F32) + l3[...].astype(F32)
    right[...] = r0[...] + r1[...].astype(F32) + r2[...].astype(F32) + r3[...].astype(F32)
    half = LEFT // 2
    for d, out in enumerate((o0, o1, o2, o3)):
        rows = pl.ds(pl.multiple_of((place[3] ^ d) * 8, 8), 8)
        out[:, :half] = jnp.concatenate([left[rows, :half], left[rows, half:]], axis=0).astype(out.dtype)
        block = right[rows, RIGHT:]
        block = jnp.concatenate([block, jnp.zeros((8, RIGHT - TABLE), F32)], axis=1)
        out[:, half:] = jnp.concatenate([right[rows, :RIGHT], block], axis=0).astype(out.dtype)


def last_kernel(a, b, c, d, qkv_o, wout_o, b_o, gain_o, table_o):
    total = a[...] + b[...].astype(F32) + c[...].astype(F32) + d[...].astype(F32)
    half = LEFT // 2
    qkv_o[:, :half] = total[:8, :half]
    qkv_o[:, half:] = total[8:, :half]
    wout_o[...] = total[:8, half : half + WIDTH]
    b_o[:, 0, :] = total[:8, half + WIDTH : half + 2 * WIDTH]
    gain_o[...] = total[:8, half + 2 * WIDTH :]
    for r in range(16):
        table_o[:, r, :] = total[8:, half + r * 128 : half + (r + 1) * 128]


def temporal_kernel(place, keeps, goes, p0, p1, p2, p3, w_in, out, grad):
    for dy, p in enumerate((p0, p1, p2, p3)):
        grad[dy * 192 : (dy + 1) * 192, :] = dot(p[...], w_in[...], NT).astype(BF16)
    slots = iota((AUDIO, BLOCK), 0)

    def of_device(x, y):
        at = ((y ^ place[3]) * 4 + (x ^ place[2])) * AUDIO
        return grad[pl.ds(pl.multiple_of(at, AUDIO), AUDIO), :]

    for b in range(TPS):
        x, y = b // 4, b % 4
        mine = dot(ones_where(keeps[b : b + 1] == slots), of_device(x, y), TN)
        theirs = dot(ones_where(goes[b : b + 1] == slots), of_device(x ^ 2, y), TN)
        out[b * BLOCK : (b + 1) * BLOCK, :] = (mine + theirs).astype(BF16)


def swap(x, axis, n, d):
    return lax.ppermute(x, axis, [(i, i ^ d) for i in range(n)])


def swaps(parts, axis):
    return (parts[0],) + tuple(swap(parts[d], axis, 4, d) for d in (1, 2, 3))


def after(x, *others):
    return lax.optimization_barrier((x,) + others)[0]


def to_all(x, axes):
    return lax.all_to_all(x, axes, 0, 0, tiled=True)


def local(
    temporal, w_in, audio_mask, counts, codes, cotangent, norm_gain, w_qkv, w_out, adapter_a, adapter_b
):
    x_at, y_at = lax.axis_index("x"), lax.axis_index("y")
    z_at, c_at = lax.axis_index("z"), lax.axis_index("c")
    place = jnp.stack([z_at, c_at, x_at, y_at, x_at * 4 + y_at]).astype(I32)
    mask = audio_mask.reshape(TPS, BLOCK)
    cot_rows = cotangent.reshape(BLOCK * BOOKS, WIDTH)
    gain = norm_gain.reshape(1, WIDTH)

    group = 4 * AUDIO
    *parts, chosen, keeps, goes, code_leave = call(
        project_kernel, "project",
        (shaped(group, WIDTH, dtype=F32),) + (shaped(group, WIDTH),) * 3
        + (shaped(TPS * AUDIO, 256), shaped(TPS, BLOCK, dtype=I32), shaped(TPS, BLOCK, dtype=I32),
           shaped(EXTRA, BOOKS, dtype=I32)),
        (place, mask, temporal, w_in, codes), scalars=1, scratch=[pltpu.VMEM((group, 256), BF16)],
    )
    code_come = swap(code_leave, "x", 4, 2)
    near = [swap(parts[d], "y", 4, d) for d in (1, 3)]
    cot_leave = call(
        leave_kernel, "leave", shaped(EXTRA * BOOKS, WIDTH), (after(place, chosen), mask, cot_rows), scalars=1,
    )
    far, cot_leave, code_come, *near = lax.optimization_barrier((parts[2], cot_leave, code_come, *near))
    parts = (parts[0], near[0], swap(far, "y", 4, 2), near[1])
    cot_come = swap(cot_leave, "x", 4, 2)
    tokens, low, embedded = call(
        embed_kernel, "embed",
        (shaped(AUDIO, BOOKS, dtype=I32), shaped(ROWS, RANK), shaped(ROWS, WIDTH, dtype=F32)),
        (after(place, code_come), mask, codes, code_come, adapter_a, adapter_b), scalars=1,
    )
    parts = call(
        project_meet_kernel, "project_meet", (shaped(AUDIO, WIDTH, dtype=F32),) + (shaped(AUDIO, WIDTH),) * 3,
        (after(place, low),) + parts, scalars=1, scratch=[pltpu.VMEM((group, WIDTH), F32)],
    )
    parts = swaps(parts, "x")
    cot, weights, grad_low, grad_mixed = call(
        upstream_kernel, "upstream",
        (shaped(ROWS, WIDTH), shaped(ROWS, 128, dtype=F32), shaped(ROWS, WIDTH), shaped(ROWS, WIDTH)),
        (after(place, parts[0]), mask, cot_rows, cot_come, w_out), scalars=1,
    )
    normed, mixed, packed, stream, inv, probs = call(
        forward_kernel, "forward",
        (shaped(ROWS, WIDTH), shaped(ROWS, WIDTH), shaped(ROWS, 3 * WIDTH),
         shaped(ROWS, WIDTH, dtype=F32), shaped(ROWS, 128, dtype=F32),
         shaped(HEADS // 2 * ROWS, 256, dtype=F32)),
        (*parts, embedded, after(gain, grad_mixed), w_qkv), limit=16,
    )
    grad_packed, give = call(
        backward_give_kernel, "backward", (shaped(ROWS, 3 * WIDTH), shaped(4, 128, LEFT)),
        (place, packed, probs, grad_mixed, normed), scalars=1,
        scratch=[pltpu.VMEM((512, ROWS), BF16)], limit=12,
    )
    got_left = swap(give, "c", 2, 1)
    message, stream_low, gain_col, give_late = call(
        norm_give_kernel, "norm",
        (shaped(2 * AUDIO, WIDTH + RANK), shaped(ROWS, WIDTH), shaped(WIDTH, 128, dtype=F32), shaped(4, 128, RIGHT)),
        (place, grad_packed, w_qkv, stream, inv, cot, weights, gain, adapter_b, tokens, mixed, grad_low, low),
        scalars=1, scratch=[pltpu.VMEM((ROWS, WIDTH), F32), pltpu.VMEM((512, ROWS), BF16)], limit=16,
    )
    got_late = swap(give_late, "c", 2, 1)
    messages = swaps((message,) * 4, "x")
    lefts = call(
        keep_left_kernel, "keep_left",
        (shaped(128, LEFT, dtype=F32),) + (shaped(128, LEFT),) * 3,
        (after(place, message), normed, grad_packed, got_left), scalars=1,
        scratch=[pltpu.VMEM((512, ROWS), BF16)],
    )
    rights = call(
        keep_right_kernel, "keep_right",
        (shaped(4, 32, RIGHT, dtype=F32),) + (shaped(4, 32, RIGHT),) * 3,
        (after(place, lefts[1]), mixed, grad_low, low, stream_low, gain_col, got_late),
        scalars=1, scratch=[pltpu.VMEM((512, ROWS), BF16), pltpu.VMEM((128, 512), F32)],
    )
    give_table, keep_table = call(
        table_kernel, "table",
        (shaped(4, 32, TABLE), shaped(4, 32, TABLE, dtype=F32)),
        (after(place, rights[1]),) + messages, scalars=1, scratch=[pltpu.VMEM((BOOKS * 512, 128), F32)],
    )
    got_table = swap(give_table, "c", 2, 1)
    near = [swap(lefts[d], "z", 4, d) for d in (1, 3)] + [swap(rights[d], "x", 4, d) for d in (1, 3)]
    piece = jnp.concatenate([m[:AUDIO, :WIDTH] for m in messages], axis=0)
    far_left, far_right, piece, got_table, *near = lax.optimization_barrier(
        (lefts[2], rights[2], piece, got_table, *near)
    )
    far_left, far_right = swap(far_left, "z", 4, 2), swap(far_right, "x", 4, 2)
    lefts = (lefts[0], near[0], far_left, near[1])
    rights = (rights[0], near[2], far_right, near[3])
    pieces = swaps((piece,) * 4, "y")
    rights = call(
        right_kernel, "right", (shaped(32, RIGHT + TABLE, dtype=F32),) + (shaped(32, RIGHT + TABLE),) * 3,
        (place,) + rights + (keep_table, got_table), scalars=1,
    )
    rights = swaps(rights, "z")
    lefts = call(
        left_kernel, "left", (shaped(32, LEFT, dtype=F32),) + (shaped(32, LEFT),) * 3,
        (place,) + lefts, scalars=1, scratch=[pltpu.VMEM((128, LEFT), F32)],
    )
    lefts = swaps(lefts, "x")
    give_win, keep_win = call(
        win_kernel, "win", (shaped(4, 256, 128), shaped(4, 256, 128, dtype=F32)),
        (place,) + pieces + (chosen,), scalars=1,
        scratch=[pltpu.VMEM((TPS * AUDIO, 256), BF16), pltpu.VMEM((TPS * AUDIO, WIDTH), BF16)],
    )
    got_win = swap(give_win, "c", 2, 1)
    wins = call(
        win_meet_kernel, "win_meet", (shaped(256, 128, dtype=F32),) + (shaped(256, 128),) * 3,
        (place, keep_win, got_win), scalars=1,
    )
    wins = swaps(wins, "z")
    columns = LEFT // 2 + RIGHT
    meets = call(
        meet_kernel, "meet", (shaped(16, columns, dtype=F32),) + (shaped(16, columns),) * 3,
        (place,) + lefts + rights, scalars=1,
        scratch=[pltpu.VMEM((32, LEFT), F32), pltpu.VMEM((32, RIGHT + TABLE), F32)],
    )
    grad_temporal = call(
        temporal_kernel, "temporal", shaped(TPS * BLOCK, 256),
        (after(place, meets[1]), keeps, goes) + pieces + (w_in,), scalars=1,
        scratch=[pltpu.VMEM((TPS * AUDIO, 256), BF16)],
    )
    meets = swaps(meets, "y")
    grad_win = wins[0] + wins[1].astype(F32) + wins[2].astype(F32) + wins[3].astype(F32)
    grad_wqkv, grad_wout, grad_b, grad_gain, grad_a = call(
        last_kernel, "last",
        (shaped(8, LEFT, dtype=F32), shaped(8, WIDTH, dtype=F32), shaped(BOOKS, 1, WIDTH, dtype=F32),
         shaped(8, GAIN, dtype=F32), shaped(BOOKS, 16, RANK, dtype=F32)),
        meets,
    )
    return (
        grad_temporal,
        grad_win,
        grad_gain[:, 0],
        grad_wqkv,
        grad_wout,
        grad_a,
        grad_b,
    )


def solution(mesh):
    grid = Mesh(mesh.devices.reshape(4, 2, 4, 4), ("z", "c", "x", "y"))
    seq, tp = ("z", "c"), ("x", "y")
    every = seq + tp
    placed = (
        P(seq, tp),
        P(tp, None),
        P(seq),
        P(),
        P(every, None),
        P(every, None, None),
        P(),
        P(),
        P(),
        P(),
        P(),
    )
    return jax.shard_map(
        local,
        mesh=grid,
        in_specs=placed,
        out_specs=(
            P(seq, tp),
            P(tp, seq),
            P(every),
            P(every, None),
            P(every, None),
            P(None, every, None),
            P(None, every, None),
        ),
        check_vma=False,
    )
```
